512 devices in a mesh: blk: 128 (over y, x, z_lo, core), inner: 4 (over z_hi).
Axes of the slice: x: 4, y: 4, z: 16 (z_hi: 4, z_lo: 4; z = z_hi * 4 + z_lo), core: 2. Of those that a mesh axis runs over, the one named last changes fastest.
Arguments:
- query_latent: bfloat16 [16384, 16384], P('blk', 'inner'), may hold values from -100 to 100
- query_rotary: bfloat16 [16384, 2048], P('blk', 'inner'), may hold values from -100 to 100
- upstream: bfloat16 [16384, 16384], P('blk', 'inner'), may hold values from -6 to 6
- latent: bfloat16 [16384, 512], P(('blk', 'inner')), may hold values from -8 to 8
- key_rotary: bfloat16 [16384, 64], P(('blk', 'inner')), may hold values from -8 to 8
- pattern: int32 [128, 6], P('blk'), may hold values from -1 to 127, as said below
Outputs:
- query_cotangent: bfloat16 [16384, 16384], P('blk', 'inner')
- rotary_cotangent: bfloat16 [16384, 2048], P('blk', 'inner')
- latent_cotangent: float32 [16384, 512], P(('blk', 'inner'))
- positional_cotangent: float32 [16384, 64], P(('blk', 'inner'))
The draws below stay inside these ranges and needn't reach their ends.
Inputs may be any that keep to these rules, and one draw needn't show every extreme that they name: `pattern`: let d_0 < d_1 < ... be the distinct numbers among 0 to 1 and m * 16 for m = 1 to 4; there are 6 of them. Entry k of row q is either q - d_k or -1, and it is -1 whenever q - d_k < 0. Entry 0 of every row is q.
All inputs are finite; a program needn't handle non-finite values.
Results may differ from the reference program's by a relative error of at most 0.0085.
Values may be sent and summed in bfloat16 or wider, within the bound.
A program may use at most 128 MiB of HBM per device.

```python
import jax
import jax.numpy as jnp
from jax import lax

HEADS = 32
LATENT = 512
ROPE = 64
NOPE = 128
BLOCK = 128
WIN = 2
NSTR = 4
NB = 128
STRIDE = 16
KMAX = 6
NTOK = 16384


def spacing_draw():
    listed = set(range(WIN))
    for number in range(1, NSTR + 1):
        listed.add(number * STRIDE)
    return sorted(listed)


def key_values(key):
    key_table = jnp.clip(jax.random.normal(jax.random.fold_in(key, 11), (NTOK, LATENT + ROPE), jnp.float32), -6.0, 6.0)
    return key_table


def query_values(key, salt, width):
    values = jnp.clip(jax.random.normal(jax.random.fold_in(key, salt), (NTOK, HEADS, width), jnp.float32), -6.0, 6.0)
    return values.reshape(NTOK, HEADS * width)


def draw_query_latent(key, part):
    return query_values(key, 21, LATENT).astype(jnp.bfloat16)


def draw_query_rotary(key, part):
    return query_values(key, 22, ROPE).astype(jnp.bfloat16)


def draw_latent(key, part):
    key_table = key_values(key)
    return key_table[:, :LATENT].astype(jnp.bfloat16)


def draw_key_rotary(key, part):
    key_table = key_values(key)
    return key_table[:, LATENT:].astype(jnp.bfloat16)


def draw_pattern(key, part):
    spacing = jnp.array(spacing_draw(), dtype=jnp.int32)[None, :]
    picks = jax.random.randint(jax.random.fold_in(key, 31), (NB, KMAX), 0, 2)
    block_rows = jnp.arange(NB, dtype=jnp.int32)[:, None]
    keeping = (spacing < WIN) | (picks == 1)
    inside = block_rows - spacing >= 0
    return jnp.where(keeping & inside, block_rows - spacing, -1).astype(jnp.int32)


def block_levels(own_key, shape, cuts, low, top_value):
    loudness = 1.0
    for axis_at, shards_of in cuts:
        heights = jax.random.uniform(jax.random.fold_in(jax.random.fold_in(own_key, 6), axis_at), (shards_of,), jnp.float32, low / len(cuts), top_value / len(cuts))
        loudness = loudness * jnp.repeat(jnp.exp(heights), shape[axis_at] // shards_of).reshape((-1,) + (1,) * (len(shape) - 1 - axis_at))
    return loudness


def centred(key, shape, spread, bound, split=(), kind=jnp.bfloat16):
    result = jax.random.normal(key, shape, jnp.float32) * spread
    if len(split) > 0:
        result = block_levels(key, shape, split, -0.22, 0.18) * result
    return jnp.clip(result, min=-bound, max=bound).astype(kind)


def setup_inputs(seed: int = 0) -> dict:
    key_list = jax.random.split(jax.random.key(seed), 7)
    query_latent = draw_query_latent(jax.random.fold_in(key_list[6], 71), 0)
    query_rotary = draw_query_rotary(jax.random.fold_in(key_list[6], 71), 0)
    upstream = centred(key_list[2], (NTOK, HEADS * LATENT), 1.0, 6.0, ((0, 128), (1, 4)))
    latent = draw_latent(jax.random.fold_in(key_list[6], 71), 0)
    key_rotary = draw_key_rotary(jax.random.fold_in(key_list[6], 71), 0)
    pattern = draw_pattern(jax.random.fold_in(key_list[6], 71), 0)
    return dict(query_latent=query_latent, query_rotary=query_rotary, upstream=upstream, latent=latent, key_rotary=key_rotary, pattern=pattern)


def spacing_list():
    listed = set(range(WIN))
    for number in range(1, NSTR + 1):
        listed.add(number * STRIDE)
    return sorted(listed)


def reference(query_latent, query_rotary, upstream, latent, key_rotary, pattern):
    softmax_scale = (NOPE + ROPE) ** -0.5
    spacing = spacing_list()
    query_blocks = query_latent.reshape(NB, BLOCK, HEADS, LATENT)
    rotary_blocks = query_rotary.reshape(NB, BLOCK, HEADS, ROPE)
    upstream_blocks = upstream.reshape(NB, BLOCK, HEADS, LATENT)
    latent_blocks = latent.reshape(NB, BLOCK, LATENT)
    rotary_keys = key_rotary.reshape(NB, BLOCK, ROPE)
    offsets = jnp.array(spacing, dtype=jnp.int32)
    position = jnp.arange(BLOCK, dtype=jnp.int32)
    causal = position[None, :] <= position[:, None]
    diagonal = offsets == 0

    def one_block(running_state, inputs):
        latent_acc, rotary_acc = running_state
        block_index, query_block, rotary_block, upward, listed = inputs
        sources = jnp.clip(block_index - offsets, 0, NB - 1).astype(jnp.int32)
        key_block = latent_blocks[sources].astype(jnp.float32)
        rope_block = rotary_keys[sources].astype(jnp.float32)
        query_full = query_block.astype(jnp.float32)
        rotary_full = rotary_block.astype(jnp.float32)
        upward_full = upward.astype(jnp.float32)
        scores = (jnp.einsum('thl,kul->thku', query_full, key_block)
                  + jnp.einsum('thr,kur->thku', rotary_full, rope_block)) * softmax_scale
        allowed = (listed >= 0)[None, None, :, None] & (causal[:, None, None, :] | ~diagonal[None, None, :, None])
        scores = jnp.where(allowed, scores, -jnp.inf)
        row_peak = jnp.max(scores, axis=(2, 3))
        log_total = row_peak + jnp.log(jnp.sum(jnp.exp(scores - row_peak[:, :, None, None]), axis=(2, 3)))
        weights = jnp.where(allowed, jnp.exp(scores - log_total[:, :, None, None]), 0.0)
        dprobs = jnp.einsum('thl,kul->thku', upward_full, key_block)
        correction = jnp.sum(weights * dprobs, axis=(2, 3))
        dscores = weights * (dprobs - correction[:, :, None, None])
        query_cot = (softmax_scale * jnp.einsum('thku,kul->thl', dscores, key_block)).astype(jnp.bfloat16)
        rotary_cot = (softmax_scale * jnp.einsum('thku,kur->thr', dscores, rope_block)).astype(jnp.bfloat16)
        key_part = (softmax_scale * jnp.einsum('thku,thl->kul', dscores, query_full)
                    + jnp.einsum('thku,thl->kul', weights, upward_full))
        rope_part = softmax_scale * jnp.einsum('thku,thr->kur', dscores, rotary_full)
        latent_acc = latent_acc.at[sources].add(key_part)
        rotary_acc = rotary_acc.at[sources].add(rope_part)
        return (latent_acc, rotary_acc), (query_cot, rotary_cot)

    initial = (jnp.zeros((NB, BLOCK, LATENT), jnp.float32), jnp.zeros((NB, BLOCK, ROPE), jnp.float32))
    block_ids = jnp.arange(NB, dtype=jnp.int32)
    (latent_acc, rotary_acc), (query_cot, rotary_cot) = lax.scan(
        one_block, initial, (block_ids, query_blocks, rotary_blocks, upstream_blocks, pattern))
    return (query_cot.reshape(NTOK, HEADS * LATENT), rotary_cot.reshape(NTOK, HEADS * ROPE),
            latent_acc.reshape(NTOK, LATENT), rotary_acc.reshape(NTOK, ROPE))
```

```python
import functools

import jax
import jax.numpy as jnp
from jax import lax
from jax.experimental import pallas as pl
from jax.experimental.pallas import tpu as pltpu
from jax.sharding import PartitionSpec as P

MESH = pl.DeviceIdType.MESH
LATENT = 512
ROPE = 64
NOPE = 128
WIN = 2
NSTR = 4
LOG2E = 1.4426950408889634
MASKED = -1e30
SLOT_ORDER = (0, 1, 3, 2)
GRAD_ORDER = (2, 1, 3, 0)


def spacing_list(blocks):
    spacing = blocks // 8
    listed = set(range(WIN))
    for number in range(1, NSTR + 1):
        listed.add(number * spacing)
    return sorted(listed)


def kernel(
    blocks,
    groups,
    spacing,
    scale,
    q_hbm,
    qr_hbm,
    up_hbm,
    lat_ref,
    kr_ref,
    pat_ref,
    qc_ref,
    rc_ref,
    lc_ref,
    pc_ref,
    qcat,
    upcat,
    qrraw,
    kbuf,
    kcat,
    s_buf,
    dp_buf,
    ds_buf,
    w_buf,
    gsend,
    gown,
    gbuf,
    rsend,
    rown,
    rbuf,
    load_sem,
    in_send,
    in_recv,
    k_send,
    k_recv,
    g_send,
    g_recv,
    r_send,
    r_recv,
):
    b = lax.axis_index("blk")
    i = lax.axis_index("inner")
    nd = len(spacing)
    heads = q_hbm.shape[1] // LATENT
    tokens = q_hbm.shape[0]
    rows = heads * tokens
    tile = lat_ref.shape[0]
    half = tile // 2
    per_slot = nd * tile

    def inner_peer(k):
        return (b, lax.rem(i + k, groups))

    def blk_peer(d):
        return (lax.rem(b + d + blocks, blocks), i)

    barrier = pltpu.get_barrier_semaphore()
    partners = {d for d in spacing if d > 0} | {(-d) % blocks for d in spacing if d > 0}
    partners = sorted(partners)
    for k in range(1, groups):
        pl.semaphore_signal(barrier, inc=1, device_id=inner_peer(k), device_id_type=MESH)
    for d in partners:
        pl.semaphore_signal(barrier, inc=1, device_id=blk_peer(d), device_id_type=MESH)

    loads = [pltpu.make_async_copy(qr_hbm, qrraw, load_sem.at[0])]
    for h in range(heads):
        span = pl.ds(h * LATENT, LATENT)
        own = pl.ds(h * tokens, tokens)
        loads.append(
            pltpu.make_async_copy(q_hbm.at[:, span], qcat.at[own, pl.ds(0, LATENT)], load_sem.at[1 + 2 * h])
        )
        loads.append(pltpu.make_async_copy(up_hbm.at[:, span], upcat.at[own], load_sem.at[2 + 2 * h]))
    for load in loads:
        load.start()

    kbuf[0, 0, :, 0:LATENT] = lat_ref[0:half]
    kbuf[0, 0, :, LATENT : 2 * LATENT] = lat_ref[half:tile]
    kbuf[0, 0, :, 2 * LATENT :] = jnp.concatenate([kr_ref[0:half], kr_ref[half:tile]], axis=1)

    pl.semaphore_wait(barrier, groups - 1 + len(partners))

    sends = []
    for k in (2, 1, 3):
        back = (groups - k) % groups
        copy = pltpu.make_async_remote_copy(
            src_ref=kbuf.at[0, 0],
            dst_ref=kbuf.at[back, 0],
            send_sem=in_send.at[k],
            recv_sem=in_recv.at[back],
            device_id=inner_peer(k),
            device_id_type=MESH,
        )
        copy.start()
        sends.append(copy)

    def forward(k):
        for n in range(1, nd):
            copy = pltpu.make_async_remote_copy(
                src_ref=kbuf.at[k, 0],
                dst_ref=kbuf.at[k, n],
                send_sem=k_send.at[k, n],
                recv_sem=k_recv.at[k, n],
                device_id=blk_peer(spacing[n]),
                device_id_type=MESH,
            )
            copy.start()
            sends.append(copy)

    forward(0)
    for k in SLOT_ORDER[1:]:
        pltpu.make_async_remote_copy(
            src_ref=kbuf.at[0, 0],
            dst_ref=kbuf.at[k, 0],
            send_sem=in_send.at[k],
            recv_sem=in_recv.at[k],
            device_id=inner_peer(k),
            device_id_type=MESH,
        ).wait_recv()
        forward(k)

    for load in loads:
        load.wait()
    lane = lax.broadcasted_iota(jnp.int32, (tokens, 2 * ROPE), 1)
    for h in range(heads):
        pair = qrraw[:, pl.ds((h // 2) * 2 * ROPE, 2 * ROPE)]
        keep = (lane < ROPE) if h % 2 == 0 else (lane >= ROPE)
        qcat[pl.ds(h * tokens, tokens), LATENT:] = jnp.where(keep, pair, jnp.zeros_like(pair))

    bias = [jnp.where(pat_ref[0, n] >= 0, 0.0, MASKED).astype(jnp.float32) for n in range(nd)]
    factor = scale * LOG2E
    lane_half = lax.broadcasted_iota(jnp.int32, (half, 2 * ROPE), 1)
    contract_last = (((1,), (1,)), ((), ()))

    for k in SLOT_ORDER:
        for n in range(1, nd):
            pltpu.make_async_remote_copy(
                src_ref=kbuf.at[k, 0],
                dst_ref=kbuf.at[k, n],
                send_sem=k_send.at[k, n],
                recv_sem=k_recv.at[k, n],
                device_id=blk_peer(spacing[n]),
                device_id_type=MESH,
            ).wait_recv()
        base = k * per_slot
        for n in range(nd):
            start = base + n * tile
            kcat[pl.ds(start, half), 0:LATENT] = kbuf[k, n, :, 0:LATENT]
            kcat[pl.ds(start + half, half), 0:LATENT] = kbuf[k, n, :, LATENT : 2 * LATENT]
            both = kbuf[k, n, :, 2 * LATENT :].astype(jnp.float32)
            turned = pltpu.roll(both, ROPE, 1)
            kcat[pl.ds(start, half), LATENT:] = jnp.where(lane_half < ROPE, both, turned).astype(jnp.bfloat16)
            kcat[pl.ds(start + half, half), LATENT:] = jnp.where(lane_half < ROPE, turned, both).astype(jnp.bfloat16)
        keys = kcat[pl.ds(base, per_slot), :]

        def score_step(p, carry, base=base, keys=keys, k=k):
            span = pl.ds(pl.multiple_of(p * 256, 256), 256)
            s = lax.dot_general(keys, qcat[span, :], contract_last, preferred_element_type=jnp.float32) * factor
            dp = lax.dot_general(
                keys[:, 0:LATENT], upcat[span, :], contract_last, preferred_element_type=jnp.float32
            )
            dp_buf[pl.ds(base, per_slot), span] = dp
            key_token = lax.broadcasted_iota(jnp.int32, (tile, 256), 0) + lax.rem(i + k, groups) * tile
            row_token = lax.rem(lax.broadcasted_iota(jnp.int32, (tile, 256), 1), tokens)
            for n in range(nd):
                part = s[n * tile : (n + 1) * tile]
                if n == 0:
                    part = jnp.where(key_token <= row_token, part, MASKED)
                else:
                    part = part + bias[n]
                s_buf[pl.ds(base + n * tile, tile), span] = part
            return carry

        lax.fori_loop(0, rows // 256, score_step, 0)

    def softmax_step(p, carry):
        span = pl.ds(pl.multiple_of(p * 128, 128), 128)
        top = jnp.max(s_buf[:, span], axis=0, keepdims=True)
        e = jnp.exp2(s_buf[:, span] - top)
        total = jnp.sum(e, axis=0, keepdims=True)
        weighted = jnp.sum(e * dp_buf[:, span], axis=0, keepdims=True)
        inverse = 1.0 / total
        correction = weighted * inverse
        w = e * inverse
        w_buf[:, span] = w.astype(jnp.bfloat16)
        ds_buf[:, span] = (w * ((dp_buf[:, span] - correction) * scale)).astype(jnp.bfloat16)
        return carry

    lax.fori_loop(0, rows // 128, softmax_step, 0)

    natural = (((1,), (0,)), ((), ()))

    def pack_rows(g, n):
        lo = g[n * tile : n * tile + half]
        hi = g[n * tile + half : (n + 1) * tile]
        rlo = lo[:, LATENT:]
        rhi = hi[:, LATENT:]
        rlo = rlo + pltpu.roll(rlo, ROPE, 1)
        rhi = rhi + pltpu.roll(rhi, ROPE, 1)
        return lo[:, 0:LATENT], hi[:, 0:LATENT], jnp.where(lane_half < ROPE, rlo, rhi)

    for k in GRAD_ORDER:
        base = k * per_slot
        dsk = ds_buf[pl.ds(base, per_slot), :]
        wk = w_buf[pl.ds(base, per_slot), :]
        g_lat = lax.dot_general(dsk, qcat[:, 0:LATENT], natural, preferred_element_type=jnp.float32)
        g_lat = g_lat + lax.dot_general(wk, upcat[...], natural, preferred_element_type=jnp.float32)
        g_rot = lax.dot_general(dsk, qcat[:, LATENT:], natural, preferred_element_type=jnp.float32)
        g = jnp.concatenate([g_lat, g_rot], axis=1)
        for n in range(nd):
            lo, hi, rot = pack_rows(g, n)
            if n == 0:
                gown[k, :, 0:LATENT] = lo
                gown[k, :, LATENT : 2 * LATENT] = hi
                gown[k, :, 2 * LATENT :] = rot
            else:
                gsend[k, n, :, 0:LATENT] = lo.astype(jnp.bfloat16)
                gsend[k, n, :, LATENT : 2 * LATENT] = hi.astype(jnp.bfloat16)
                gsend[k, n, :, 2 * LATENT :] = rot.astype(jnp.bfloat16)
        for n in range(1, nd):
            copy = pltpu.make_async_remote_copy(
                src_ref=gsend.at[k, n],
                dst_ref=gbuf.at[k, n],
                send_sem=g_send.at[k, n],
                recv_sem=g_recv.at[k, n],
                device_id=blk_peer(-spacing[n]),
                device_id_type=MESH,
            )
            copy.start()
            sends.append(copy)

    lane_tok = lax.broadcasted_iota(jnp.int32, (tokens, 2 * ROPE), 1)
    for p in range(heads // 2):
        out = []
        for h in (2 * p, 2 * p + 1):
            span = pl.ds(h * tokens, tokens)
            dq = lax.dot_general(
                ds_buf[:, span], kcat[...], (((0,), (0,)), ((), ())), preferred_element_type=jnp.float32
            )
            qc_ref[:, pl.ds(h * LATENT, LATENT)] = dq[:, 0:LATENT].astype(jnp.bfloat16)
            out.append(dq[:, LATENT:])
        rc_ref[:, pl.ds(p * 2 * ROPE, 2 * ROPE)] = jnp.where(lane_tok < ROPE, out[0], out[1]).astype(jnp.bfloat16)

    for k in GRAD_ORDER:
        total = gown[k]
        for n in range(1, nd):
            pltpu.make_async_remote_copy(
                src_ref=gsend.at[k, n],
                dst_ref=gbuf.at[k, n],
                send_sem=g_send.at[k, n],
                recv_sem=g_recv.at[k, n],
                device_id=blk_peer(-spacing[n]),
                device_id_type=MESH,
            ).wait_recv()
            total = total + gbuf[k, n].astype(jnp.float32)
        if k == 0:
            rown[...] = total
        else:
            back = (groups - k) % groups
            rsend[k] = total.astype(jnp.bfloat16)
            copy = pltpu.make_async_remote_copy(
                src_ref=rsend.at[k],
                dst_ref=rbuf.at[back],
                send_sem=r_send.at[k],
                recv_sem=r_recv.at[back],
                device_id=inner_peer(k),
                device_id_type=MESH,
            )
            copy.start()
            sends.append(copy)

    total = rown[...]
    for k in range(1, groups):
        pltpu.make_async_remote_copy(
            src_ref=rsend.at[k],
            dst_ref=rbuf.at[k],
            send_sem=r_send.at[k],
            recv_sem=r_recv.at[k],
            device_id=inner_peer(k),
            device_id_type=MESH,
        ).wait_recv()
        total = total + rbuf[k].astype(jnp.float32)
    lc_ref[0:half, :] = total[:, 0:LATENT]
    lc_ref[half:tile, :] = total[:, LATENT : 2 * LATENT]
    pc_ref[0:half, :] = total[:, 2 * LATENT : 2 * LATENT + ROPE]
    pc_ref[half:tile, :] = total[:, 2 * LATENT + ROPE :]
    for copy in sends:
        copy.wait_send()


def per_device(query_latent, query_rotary, upstream, latent, key_rotary, pattern):
    blocks = lax.axis_size("blk")
    groups = lax.axis_size("inner")
    spacing = spacing_list(blocks)
    nd = len(spacing)
    scale = (NOPE + ROPE) ** (-0.5)
    tokens, width = query_latent.shape
    heads = width // LATENT
    rows = heads * tokens
    tile = latent.shape[0]
    half = tile // 2
    packed = 2 * (LATENT + ROPE)
    keys = nd * groups * tile
    vmem = pl.BlockSpec(memory_space=pltpu.VMEM)
    hbm = pl.BlockSpec(memory_space=pl.ANY)
    smem = pl.BlockSpec(memory_space=pltpu.SMEM)
    bf, f32 = jnp.bfloat16, jnp.float32
    dma = pltpu.SemaphoreType.DMA
    return pl.pallas_call(
        functools.partial(kernel, blocks, groups, spacing, scale),
        out_shape=(
            jax.ShapeDtypeStruct(query_latent.shape, bf),
            jax.ShapeDtypeStruct(query_rotary.shape, bf),
            jax.ShapeDtypeStruct(latent.shape, f32),
            jax.ShapeDtypeStruct(key_rotary.shape, f32),
        ),
        in_specs=[hbm, hbm, hbm, vmem, vmem, smem],
        out_specs=(vmem, vmem, vmem, vmem),
        scratch_shapes=[
            pltpu.VMEM((rows, LATENT + 2 * ROPE), bf),
            pltpu.VMEM((rows, LATENT), bf),
            pltpu.VMEM(query_rotary.shape, bf),
            pltpu.VMEM((groups, nd, half, packed), bf),
            pltpu.VMEM((keys, LATENT + 2 * ROPE), bf),
            pltpu.VMEM((keys, rows), f32),
            pltpu.VMEM((keys, rows), f32),
            pltpu.VMEM((keys, rows), bf),
            pltpu.VMEM((keys, rows), bf),
            pltpu.VMEM((groups, nd, half, packed), bf),
            pltpu.VMEM((groups, half, packed), f32),
            pltpu.VMEM((groups, nd, half, packed), bf),
            pltpu.VMEM((groups, half, packed), bf),
            pltpu.VMEM((half, packed), f32),
            pltpu.VMEM((groups, half, packed), bf),
            dma((1 + 2 * heads,)),
            dma((groups,)),
            dma((groups,)),
            dma((groups, nd)),
            dma((groups, nd)),
            dma((groups, nd)),
            dma((groups, nd)),
            dma((groups,)),
            dma((groups,)),
        ],
        compiler_params=pltpu.CompilerParams(
            collective_id=0, has_side_effects=True, vmem_limit_bytes=50 * 1024 * 1024
        ),
        cost_estimate=pl.CostEstimate(flops=4_300_000_000, bytes_accessed=4_000_000, transcendentals=800_000),
    )(query_latent, query_rotary, upstream, latent, key_rotary, pattern)


def solution(mesh):
    in_specs = (
        P("blk", "inner"),
        P("blk", "inner"),
        P("blk", "inner"),
        P(("blk", "inner"), None),
        P(("blk", "inner"), None),
        P("blk", None),
    )
    out_specs = (
        P("blk", "inner"),
        P("blk", "inner"),
        P(("blk", "inner"), None),
        P(("blk", "inner"), None),
    )
    return jax.shard_map(
        per_device, mesh=mesh, in_specs=in_specs, out_specs=out_specs, check_vma=False
    )
```

```python
import functools

import jax
import jax.numpy as jnp
from jax import lax
from jax.experimental import pallas as pl
from jax.experimental.pallas import tpu as pltpu
from jax.sharding import PartitionSpec as P

MESH = pl.DeviceIdType.MESH
LATENT = 512
ROPE = 64
NOPE = 128
WIN = 2
NSTR = 4
LOG2E = 1.4426950408889634
MASKED = -1e30
PLACE = {0: 0, 1: 1, 3: 2, 2: 3}
ARRIVALS = ((0,), (1, 3), (2,))
GRAD_ORDER = (2, 1, 3, 0)
RELAY_CUT = 640


def spacing_list(blocks):
    spacing = blocks // 8
    listed = set(range(WIN))
    for number in range(1, NSTR + 1):
        listed.add(number * spacing)
    return sorted(listed)


def kernel(
    blocks,
    groups,
    spacing,
    scale,
    q_hbm,
    qr_hbm,
    up_hbm,
    lat_hbm,
    kr_hbm,
    pat_hbm,
    qc_hbm,
    rc_ref,
    lc_ref,
    pc_ref,
    qcat,
    upcat,
    q_turned,
    up_turned,
    qrraw,
    lat_ref,
    kr_ref,
    pat_ref,
    kbuf,
    kcat,
    e_buf,
    dp_buf,
    ds_buf,
    w_buf,
    top_buf,
    sum_buf,
    mix_buf,
    qc_ref,
    gsend,
    gown,
    gbuf,
    rsend,
    rown,
    rbuf,
    small_sem,
    load_sem,
    out_sem,
    in_send,
    in_recv,
    k_send,
    k_recv,
    g_send,
    g_recv,
    r_send,
    r_recv,
):
    b = lax.axis_index("blk")
    i = lax.axis_index("inner")
    nd = len(spacing)
    heads = q_hbm.shape[1] // LATENT
    tokens = q_hbm.shape[0]
    rows = heads * tokens
    tile = lat_hbm.shape[0]
    half = tile // 2
    per_slot = nd * tile
    packed = kbuf.shape[3]
    bf = jnp.bfloat16
    f32 = jnp.float32

    def inner_peer(k):
        return (b, lax.rem(i + k, groups))

    def blk_peer(d):
        return (lax.rem(b + d + blocks, blocks), i)

    small = [
        pltpu.make_async_copy(lat_hbm, lat_ref, small_sem.at[0]),
        pltpu.make_async_copy(kr_hbm, kr_ref, small_sem.at[1]),
        pltpu.make_async_copy(pat_hbm, pat_ref, small_sem.at[2]),
    ]
    for load in small:
        load.start()

    barrier = pltpu.get_barrier_semaphore()
    partners = {d for d in spacing if d > 0} | {(-d) % blocks for d in spacing if d > 0}
    partners = sorted(partners)
    for k in (1, 3):
        pl.semaphore_signal(barrier, inc=1, device_id=inner_peer(k), device_id_type=MESH)
    for d in partners:
        pl.semaphore_signal(barrier, inc=1, device_id=blk_peer(d), device_id_type=MESH)

    qr_load = pltpu.make_async_copy(qr_hbm, qrraw, load_sem.at[0])
    qr_load.start()
    loads = []
    for h in range(heads):
        span = pl.ds(h * LATENT, LATENT)
        own = pl.ds(h * tokens, tokens)
        pair = (
            pltpu.make_async_copy(q_hbm.at[:, span], qcat.at[own, pl.ds(0, LATENT)], load_sem.at[1 + 2 * h]),
            pltpu.make_async_copy(up_hbm.at[:, span], upcat.at[own], load_sem.at[2 + 2 * h]),
        )
        for load in pair:
            load.start()
        loads.append(pair)

    for load in small:
        load.wait()
    kbuf[0, 0, :, 0:LATENT] = lat_ref[0:half]
    kbuf[0, 0, :, LATENT : 2 * LATENT] = lat_ref[half:tile]
    kbuf[0, 0, :, 2 * LATENT :] = jnp.concatenate([kr_ref[0:half], kr_ref[half:tile]], axis=1)

    pl.semaphore_wait(barrier, 2 + len(partners))

    sends = []

    def launch(copy):
        copy.start()
        sends.append(copy)

    def near_tile(k):
        back = groups - k
        return pltpu.make_async_remote_copy(
            src_ref=kbuf.at[0, 0],
            dst_ref=kbuf.at[back, 0],
            send_sem=in_send.at[k],
            recv_sem=in_recv.at[back],
            device_id=inner_peer(k),
            device_id_type=MESH,
        )

    def relayed_half(k, slot):
        span = pl.ds(0, RELAY_CUT) if k == 1 else pl.ds(RELAY_CUT, packed - RELAY_CUT)
        n = 0 if k == 1 else 2
        return pltpu.make_async_remote_copy(
            src_ref=kbuf.at[slot, 0, :, span],
            dst_ref=kbuf.at[2, 0, :, span],
            send_sem=in_send.at[n],
            recv_sem=in_recv.at[n],
            device_id=inner_peer(k),
            device_id_type=MESH,
        )

    def block_tile(k, n):
        return pltpu.make_async_remote_copy(
            src_ref=kbuf.at[k, 0],
            dst_ref=kbuf.at[k, n],
            send_sem=k_send.at[k, n],
            recv_sem=k_recv.at[k, n],
            device_id=blk_peer(spacing[n]),
            device_id_type=MESH,
        )

    def block_grad(k, n):
        return pltpu.make_async_remote_copy(
            src_ref=gsend.at[k, n],
            dst_ref=gbuf.at[k, n],
            send_sem=g_send.at[k, n],
            recv_sem=g_recv.at[k, n],
            device_id=blk_peer(-spacing[n]),
            device_id_type=MESH,
        )

    def inner_grad(k):
        back = groups - k
        return pltpu.make_async_remote_copy(
            src_ref=rsend.at[k],
            dst_ref=rbuf.at[back],
            send_sem=r_send.at[k],
            recv_sem=r_recv.at[back],
            device_id=inner_peer(k),
            device_id_type=MESH,
        )

    def forward(k):
        for n in (4, 5, 3, 2, 1):
            launch(block_tile(k, n))

    launch(near_tile(1))
    launch(near_tile(3))
    forward(0)

    qr_load.wait()
    lane = lax.broadcasted_iota(jnp.int32, (tokens, 2 * ROPE), 1)
    for h in range(heads):
        own = pl.ds(h * tokens, tokens)
        pair = qrraw[:, pl.ds((h // 2) * 2 * ROPE, 2 * ROPE)]
        keep = (lane < ROPE) if h % 2 == 0 else (lane >= ROPE)
        qcat[own, LATENT:] = jnp.where(keep, pair, jnp.zeros_like(pair))
        for load in loads[h]:
            load.wait()
        q_turned[:, own] = qcat[own, :].T
        up_turned[:, own] = upcat[own, :].T

    bias = [jnp.where(pat_ref[0, n] >= 0, 0.0, MASKED).astype(f32) for n in range(nd)]
    factor = scale * LOG2E
    lane_half = lax.broadcasted_iota(jnp.int32, (half, 2 * ROPE), 1)
    natural = (((1,), (0,)), ((), ()))

    def take_keys(k):
        for n in range(1, nd):
            block_tile(k, n).wait_recv()
        for n in range(nd):
            start = PLACE[k] * per_slot + n * tile
            kcat[pl.ds(start, half), 0:LATENT] = kbuf[k, n, :, 0:LATENT]
            kcat[pl.ds(start + half, half), 0:LATENT] = kbuf[k, n, :, LATENT : 2 * LATENT]
            both = kbuf[k, n, :, 2 * LATENT :].astype(f32)
            turned = pltpu.roll(both, ROPE, 1)
            kcat[pl.ds(start, half), LATENT:] = jnp.where(lane_half < ROPE, both, turned).astype(bf)
            kcat[pl.ds(start + half, half), LATENT:] = jnp.where(lane_half < ROPE, turned, both).astype(bf)

    def score(group):
        slots = ARRIVALS[group]
        base = PLACE[slots[0]] * per_slot
        count = len(slots) * per_slot
        span_rows = pl.ds(base, count)

        def step(p, carry):
            span = pl.ds(pl.multiple_of(p * 256, 256), 256)
            s = lax.dot_general(kcat[span_rows, :], q_turned[:, span], natural, preferred_element_type=f32) * factor
            dp = lax.dot_general(
                kcat[span_rows, 0:LATENT], up_turned[:, span], natural, preferred_element_type=f32
            )
            key_token = lax.broadcasted_iota(jnp.int32, (tile, 256), 0)
            row_token = lax.rem(lax.broadcasted_iota(jnp.int32, (tile, 256), 1), tokens)
            parts = []
            for m, k in enumerate(slots):
                for n in range(nd):
                    part = s[m * per_slot + n * tile : m * per_slot + (n + 1) * tile]
                    if n == 0:
                        first = lax.rem(i + k, groups) * tile
                        parts.append(jnp.where(key_token + first <= row_token, part, MASKED))
                    else:
                        parts.append(part + bias[n])
            s = jnp.concatenate(parts, axis=0)
            top = jnp.max(s, axis=0, keepdims=True)
            e = jnp.exp2(s - top)
            e_buf[span_rows, span] = e
            dp_buf[span_rows, span] = dp
            top_buf[group : group + 1, span] = top
            sum_buf[group : group + 1, span] = jnp.sum(e, axis=0, keepdims=True)
            mix_buf[group : group + 1, span] = jnp.sum(e * dp, axis=0, keepdims=True)
            return carry

        lax.fori_loop(0, rows // 256, step, 0)

    near_tile(1).wait_recv()
    launch(relayed_half(1, 3))
    near_tile(3).wait_recv()
    launch(relayed_half(3, 1))
    forward(3)
    forward(1)
    take_keys(0)
    score(0)
    relayed_half(1, 3).wait_recv()
    relayed_half(3, 1).wait_recv()
    forward(2)
    take_keys(1)
    take_keys(3)
    score(1)
    take_keys(2)
    score(2)

    tops = [top_buf[g : g + 1, :] for g in range(3)]
    top = jnp.maximum(jnp.maximum(tops[0], tops[1]), tops[2])
    fade = [jnp.exp2(t - top) for t in tops]
    total = sum(fade[g] * sum_buf[g : g + 1, :] for g in range(3))
    mix = sum(fade[g] * mix_buf[g : g + 1, :] for g in range(3))
    inverse = 1.0 / total
    mix_buf[3:4, :] = mix * inverse
    for g in range(3):
        sum_buf[4 + g : 5 + g, :] = fade[g] * inverse

    def pack_rows(g, n):
        lo = g[n * tile : n * tile + half]
        hi = g[n * tile + half : (n + 1) * tile]
        rlo = lo[:, LATENT:]
        rhi = hi[:, LATENT:]
        rlo = rlo + pltpu.roll(rlo, ROPE, 1)
        rhi = rhi + pltpu.roll(rhi, ROPE, 1)
        return lo[:, 0:LATENT], hi[:, 0:LATENT], jnp.where(lane_half < ROPE, rlo, rhi)

    for k in GRAD_ORDER:
        group = [g for g in range(3) if k in ARRIVALS[g]][0]
        span_rows = pl.ds(PLACE[k] * per_slot, per_slot)

        def weigh(p, carry, group=group, span_rows=span_rows):
            span = pl.ds(pl.multiple_of(p * 256, 256), 256)
            w = e_buf[span_rows, span] * sum_buf[4 + group : 5 + group, span]
            w_buf[span_rows, span] = w.astype(bf)
            ds_buf[span_rows, span] = (w * ((dp_buf[span_rows, span] - mix_buf[3:4, span]) * scale)).astype(bf)
            return carry

        lax.fori_loop(0, rows // 256, weigh, 0)
        dsk = ds_buf[span_rows, :]
        wk = w_buf[span_rows, :]
        g_lat = lax.dot_general(dsk, qcat[:, 0:LATENT], natural, preferred_element_type=f32)
        g_lat = g_lat + lax.dot_general(wk, upcat[...], natural, preferred_element_type=f32)
        g_rot = lax.dot_general(dsk, qcat[:, LATENT:], natural, preferred_element_type=f32)
        g = jnp.concatenate([g_lat, g_rot], axis=1)
        for n in range(nd):
            lo, hi, rot = pack_rows(g, n)
            if n == 0:
                gown[k, :, 0:LATENT] = lo
                gown[k, :, LATENT : 2 * LATENT] = hi
                gown[k, :, 2 * LATENT :] = rot
            else:
                gsend[k, n, :, 0:LATENT] = lo.astype(bf)
                gsend[k, n, :, LATENT : 2 * LATENT] = hi.astype(bf)
                gsend[k, n, :, 2 * LATENT :] = rot.astype(bf)
        for n in (4, 5, 3, 2, 1):
            launch(block_grad(k, n))

    outs = []
    lane_tok = lax.broadcasted_iota(jnp.int32, (tokens, 2 * ROPE), 1)
    for p in range(heads // 2):
        turned = []
        for h in (2 * p, 2 * p + 1):
            span = pl.ds(h * tokens, tokens)
            dq = lax.dot_general(ds_buf[:, span], kcat[...], (((0,), (0,)), ((), ())), preferred_element_type=f32)
            qc_ref[:, pl.ds(h * LATENT, LATENT)] = dq[:, 0:LATENT].astype(bf)
            turned.append(dq[:, LATENT:])
        rc_ref[:, pl.ds(p * 2 * ROPE, 2 * ROPE)] = jnp.where(lane_tok < ROPE, turned[0], turned[1]).astype(bf)
    out = pltpu.make_async_copy(qc_ref, qc_hbm, out_sem.at[0])
    out.start()

    for k in GRAD_ORDER:
        total = gown[k]
        for n in range(1, nd):
            block_grad(k, n).wait_recv()
            total = total + gbuf[k, n].astype(f32)
        if k == 0:
            rown[...] = total
        else:
            rsend[k] = total.astype(bf)
            launch(inner_grad(k))

    total = rown[...]
    for k in range(1, groups):
        inner_grad(groups - k).wait_recv()
        total = total + rbuf[k].astype(f32)
    lc_ref[0:half, :] = total[:, 0:LATENT]
    lc_ref[half:tile, :] = total[:, LATENT : 2 * LATENT]
    pc_ref[0:half, :] = total[:, 2 * LATENT : 2 * LATENT + ROPE]
    pc_ref[half:tile, :] = total[:, 2 * LATENT + ROPE :]
    for copy in sends:
        copy.wait_send()
    out.wait()


def place_results(qc_in, rc_in, lc_in, pc_in, qc_out, rc_out, lc_out, pc_out, qc_buf, rc_buf, lc_buf, pc_buf, sems):
    strip = 16
    moves = []
    for r in range(0, qc_in.shape[0], strip):
        rows = pl.ds(r, strip)
        moves.append((qc_in.at[rows], qc_buf.at[rows], qc_out.at[rows]))
    moves += [(rc_in, rc_buf, rc_out), (lc_in, lc_buf, lc_out), (pc_in, pc_buf, pc_out)]
    steps = [
        (pltpu.make_async_copy(src, mid, sems.at[0, n]), pltpu.make_async_copy(mid, dst, sems.at[1, n]))
        for n, (src, mid, dst) in enumerate(moves)
    ]
    for load, _ in steps:
        load.start()
    for load, store in steps:
        load.wait()
        store.start()
    for _, store in steps:
        store.wait()


def per_device(query_latent, query_rotary, upstream, latent, key_rotary, pattern):
    blocks = lax.axis_size("blk")
    groups = lax.axis_size("inner")
    spacing = spacing_list(blocks)
    nd = len(spacing)
    scale = (NOPE + ROPE) ** (-0.5)
    tokens, width = query_latent.shape
    heads = width // LATENT
    rows = heads * tokens
    tile = latent.shape[0]
    half = tile // 2
    packed = 2 * (LATENT + ROPE)
    keys = nd * groups * tile
    vmem = pl.BlockSpec(memory_space=pltpu.VMEM)
    hbm = pl.BlockSpec(memory_space=pltpu.HBM)
    bf, f32 = jnp.bfloat16, jnp.float32
    dma = pltpu.SemaphoreType.DMA
    outs = pl.pallas_call(
        functools.partial(kernel, blocks, groups, spacing, scale),
        out_shape=(
            jax.ShapeDtypeStruct(query_latent.shape, bf),
            jax.ShapeDtypeStruct(query_rotary.shape, bf),
            jax.ShapeDtypeStruct(latent.shape, f32),
            jax.ShapeDtypeStruct(key_rotary.shape, f32),
        ),
        in_specs=[hbm] * 6,
        out_specs=(hbm, vmem, vmem, vmem),
        scratch_shapes=[
            pltpu.VMEM((rows, LATENT + 2 * ROPE), bf),
            pltpu.VMEM((rows, LATENT), bf),
            pltpu.VMEM((LATENT + 2 * ROPE, rows), bf),
            pltpu.VMEM((LATENT, rows), bf),
            pltpu.VMEM(query_rotary.shape, bf),
            pltpu.VMEM(latent.shape, bf),
            pltpu.VMEM(key_rotary.shape, bf),
            pltpu.SMEM(pattern.shape, jnp.int32),
            pltpu.VMEM((groups, nd, half, packed), bf),
            pltpu.VMEM((keys, LATENT + 2 * ROPE), bf),
            pltpu.VMEM((keys, rows), f32),
            pltpu.VMEM((keys, rows), f32),
            pltpu.VMEM((keys, rows), bf),
            pltpu.VMEM((keys, rows), bf),
            pltpu.VMEM((8, rows), f32),
            pltpu.VMEM((8, rows), f32),
            pltpu.VMEM((8, rows), f32),
            pltpu.VMEM(query_latent.shape, bf),
            pltpu.VMEM((groups, nd, half, packed), bf),
            pltpu.VMEM((groups, half, packed), f32),
            pltpu.VMEM((groups, nd, half, packed), bf),
            pltpu.VMEM((groups, half, packed), bf),
            pltpu.VMEM((half, packed), f32),
            pltpu.VMEM((groups, half, packed), bf),
            dma((3,)),
            dma((1 + 2 * heads,)),
            dma((1,)),
            dma((groups,)),
            dma((groups,)),
            dma((groups, nd)),
            dma((groups, nd)),
            dma((groups, nd)),
            dma((groups, nd)),
            dma((groups,)),
            dma((groups,)),
        ],
        compiler_params=pltpu.CompilerParams(
            collective_id=0, has_side_effects=True, vmem_limit_bytes=60 * 1024 * 1024
        ),
        cost_estimate=pl.CostEstimate(flops=4_300_000_000, bytes_accessed=4_000_000, transcendentals=800_000),
    )(query_latent, query_rotary, upstream, latent, key_rotary, pattern)
    return pl.pallas_call(
        place_results,
        out_shape=tuple(jax.ShapeDtypeStruct(x.shape, x.dtype) for x in outs),
        in_specs=[hbm] * 4,
        out_specs=tuple([hbm] * 4),
        scratch_shapes=[pltpu.VMEM(x.shape, x.dtype) for x in outs] + [dma((2, tokens // 16 + 3))],
        compiler_params=pltpu.CompilerParams(vmem_limit_bytes=60 * 1024 * 1024),
    )(*outs)


def solution(mesh):
    in_specs = (
        P("blk", "inner"),
        P("blk", "inner"),
        P("blk", "inner"),
        P(("blk", "inner"), None),
        P(("blk", "inner"), None),
        P("blk", None),
    )
    out_specs = (
        P("blk", "inner"),
        P("blk", "inner"),
        P(("blk", "inner"), None),
        P(("blk", "inner"), None),
    )
    return jax.shard_map(
        per_device, mesh=mesh, in_specs=in_specs, out_specs=out_specs, check_vma=False
    )
```

```python
import functools

import jax
import jax.numpy as jnp
from jax import lax
from jax.experimental import pallas as pl
from jax.experimental.pallas import tpu as pltpu
from jax.sharding import PartitionSpec as P

MESH = pl.DeviceIdType.MESH
LATENT = 512
ROPE = 64
NOPE = 128
WIN = 2
NSTR = 4
LOG2E = 1.4426950408889634
MASKED = -1e30
PLACE = {0: 0, 1: 1, 3: 2, 2: 3}
ARRIVALS = ((0,), (1, 3), (2,))
RELAY_CUT = 640


def spacing_list(blocks):
    spacing = blocks // 8
    listed = set(range(WIN))
    for number in range(1, NSTR + 1):
        listed.add(number * spacing)
    return sorted(listed)


def kernel(
    blocks,
    groups,
    spacing,
    scale,
    q_hbm,
    qr_hbm,
    up_hbm,
    lat_hbm,
    kr_hbm,
    pat_hbm,
    qc_ref,
    rc_ref,
    lc_ref,
    pc_ref,
    qcat,
    upcat,
    q_turned,
    up_turned,
    qrraw,
    lat_ref,
    kr_ref,
    pat_ref,
    kbuf,
    kcat,
    e_buf,
    dp_buf,
    ds_buf,
    w_buf,
    top_buf,
    sum_buf,
    mix_buf,
    norm_buf,
    gsend,
    gown,
    gbuf,
    rsend,
    rown,
    rbuf,
    small_sem,
    load_sem,
    in_send,
    in_recv,
    k_send,
    k_recv,
    g_send,
    g_recv,
    r_send,
    r_recv,
):
    b = lax.axis_index("blk")
    i = lax.axis_index("inner")
    nd = len(spacing)
    heads = q_hbm.shape[1] // LATENT
    tokens = q_hbm.shape[0]
    rows = heads * tokens
    tile = lat_hbm.shape[0]
    half = tile // 2
    per_slot = nd * tile
    packed = kbuf.shape[3]
    bf = jnp.bfloat16
    f32 = jnp.float32

    def inner_peer(k):
        return (b, lax.rem(i + k, groups))

    def blk_peer(d):
        return (lax.rem(b + d + blocks, blocks), i)

    small = [
        pltpu.make_async_copy(lat_hbm, lat_ref, small_sem.at[0]),
        pltpu.make_async_copy(kr_hbm, kr_ref, small_sem.at[1]),
        pltpu.make_async_copy(pat_hbm, pat_ref, small_sem.at[2]),
    ]
    barrier = pltpu.get_barrier_semaphore()
    partners = {d for d in spacing if d > 0} | {(-d) % blocks for d in spacing if d > 0}
    partners = sorted(partners)
    for k in (1, 3):
        pl.semaphore_signal(barrier, inc=1, device_id=inner_peer(k), device_id_type=MESH)
    for d in partners:
        pl.semaphore_signal(barrier, inc=1, device_id=blk_peer(d), device_id_type=MESH)

    for load in small:
        load.start()
    qr_load = pltpu.make_async_copy(qr_hbm, qrraw, load_sem.at[0])
    qr_load.start()
    loads = []
    for h in range(heads):
        span = pl.ds(h * LATENT, LATENT)
        own = pl.ds(h * tokens, tokens)
        pair = (
            pltpu.make_async_copy(q_hbm.at[:, span], qcat.at[own, pl.ds(0, LATENT)], load_sem.at[1 + 2 * h]),
            pltpu.make_async_copy(up_hbm.at[:, span], upcat.at[own], load_sem.at[2 + 2 * h]),
        )
        for load in pair:
            load.start()
        loads.append(pair)

    for load in small:
        load.wait()
    kbuf[0, 0, :, 0:LATENT] = lat_ref[0:half]
    kbuf[0, 0, :, LATENT : 2 * LATENT] = lat_ref[half:tile]
    kbuf[0, 0, :, 2 * LATENT :] = jnp.concatenate([kr_ref[0:half], kr_ref[half:tile]], axis=1)

    pl.semaphore_wait(barrier, 2 + len(partners))

    sends = []

    def launch(copy):
        copy.start()
        sends.append(copy)

    spans = (pl.ds(0, RELAY_CUT), pl.ds(RELAY_CUT, packed - RELAY_CUT))

    def inner_half(n, k, part, source, target):
        return pltpu.make_async_remote_copy(
            src_ref=kbuf.at[source, 0, :, spans[part]],
            dst_ref=kbuf.at[target, 0, :, spans[part]],
            send_sem=in_send.at[n],
            recv_sem=in_recv.at[n],
            device_id=inner_peer(k),
            device_id_type=MESH,
        )

    near_first = (inner_half(0, 1, 0, 0, 3), inner_half(1, 3, 1, 0, 1))
    near_second = (inner_half(2, 1, 1, 0, 3), inner_half(3, 3, 0, 0, 1))
    relayed = (inner_half(4, 1, 0, 3, 2), inner_half(5, 3, 1, 1, 2))

    def block_tile(k, n):
        return pltpu.make_async_remote_copy(
            src_ref=kbuf.at[k, 0],
            dst_ref=kbuf.at[k, n],
            send_sem=k_send.at[k, n],
            recv_sem=k_recv.at[k, n],
            device_id=blk_peer(spacing[n]),
            device_id_type=MESH,
        )

    def block_grad(k, n):
        return pltpu.make_async_remote_copy(
            src_ref=gsend.at[k, n],
            dst_ref=gbuf.at[k, n],
            send_sem=g_send.at[k, n],
            recv_sem=g_recv.at[k, n],
            device_id=blk_peer(-spacing[n]),
            device_id_type=MESH,
        )

    def inner_grad(k):
        back = lax.rem(groups - k, groups)
        return pltpu.make_async_remote_copy(
            src_ref=rsend.at[k],
            dst_ref=rbuf.at[back],
            send_sem=r_send.at[k],
            recv_sem=r_recv.at[back],
            device_id=inner_peer(k),
            device_id_type=MESH,
        )

    def forward(k):
        for n in (4, 5, 3, 2, 1):
            launch(block_tile(k, n))

    for copy in near_first + near_second:
        launch(copy)
    forward(0)

    qr_load.wait()
    lane = lax.broadcasted_iota(jnp.int32, (tokens, 2 * ROPE), 1)
    for h in range(heads):
        own = pl.ds(h * tokens, tokens)
        pair = qrraw[:, pl.ds((h // 2) * 2 * ROPE, 2 * ROPE)]
        keep = (lane < ROPE) if h % 2 == 0 else (lane >= ROPE)
        qcat[own, LATENT:] = jnp.where(keep, pair, jnp.zeros_like(pair))
        for load in loads[h]:
            load.wait()
        q_turned[:, own] = qcat[own, :].T
        up_turned[:, own] = upcat[own, :].T

    bias = [jnp.where(pat_ref[0, n] >= 0, 0.0, MASKED).astype(f32) for n in range(nd)]
    factor = scale * LOG2E
    lane_half = lax.broadcasted_iota(jnp.int32, (half, 2 * ROPE), 1)
    natural = (((1,), (0,)), ((), ()))

    def take_keys(k):
        for n in range(1, nd):
            block_tile(k, n).wait_recv()
        for n in range(nd):
            start = PLACE[k] * per_slot + n * tile
            kcat[pl.ds(start, half), 0:LATENT] = kbuf[k, n, :, 0:LATENT]
            kcat[pl.ds(start + half, half), 0:LATENT] = kbuf[k, n, :, LATENT : 2 * LATENT]
            both = kbuf[k, n, :, 2 * LATENT :].astype(f32)
            turned = pltpu.roll(both, ROPE, 1)
            kcat[pl.ds(start, half), LATENT:] = jnp.where(lane_half < ROPE, both, turned).astype(bf)
            kcat[pl.ds(start + half, half), LATENT:] = jnp.where(lane_half < ROPE, turned, both).astype(bf)

    def score(group):
        slots = ARRIVALS[group]
        base = PLACE[slots[0]] * per_slot
        count = len(slots) * per_slot
        span_rows = pl.ds(base, count)

        def step(p, carry):
            span = pl.ds(pl.multiple_of(p * 256, 256), 256)
            s = lax.dot_general(kcat[span_rows, :], q_turned[:, span], natural, preferred_element_type=f32) * factor
            dp = lax.dot_general(
                kcat[span_rows, 0:LATENT], up_turned[:, span], natural, preferred_element_type=f32
            )
            key_token = lax.broadcasted_iota(jnp.int32, (tile, 256), 0)
            row_token = lax.rem(lax.broadcasted_iota(jnp.int32, (tile, 256), 1), tokens)
            parts = []
            for m, k in enumerate(slots):
                for n in range(nd):
                    part = s[m * per_slot + n * tile : m * per_slot + (n + 1) * tile]
                    if n == 0:
                        first = lax.rem(i + k, groups) * tile
                        parts.append(jnp.where(key_token + first <= row_token, part, MASKED))
                    else:
                        parts.append(part + bias[n])
            s = jnp.concatenate(parts, axis=0)
            top = jnp.max(s, axis=0, keepdims=True)
            e = jnp.exp2(s - top)
            e_buf[span_rows, span] = e
            dp_buf[span_rows, span] = dp
            top_buf[group : group + 1, span] = top
            sum_buf[group : group + 1, span] = jnp.sum(e, axis=0, keepdims=True)
            mix_buf[group : group + 1, span] = jnp.sum(e * dp, axis=0, keepdims=True)
            return carry

        lax.fori_loop(0, rows // 256, step, 0, unroll=True)

    for n in range(2):
        near_first[n].wait_recv()
        launch(relayed[n])
    for n in range(2):
        near_second[n].wait_recv()
        forward(3 - 2 * n)
    take_keys(0)
    score(0)
    for copy in relayed:
        copy.wait_recv()
    forward(2)
    take_keys(1)
    take_keys(3)
    score(1)
    take_keys(2)
    score(2)

    tops = [top_buf[g : g + 1, :] for g in range(3)]
    top = jnp.maximum(jnp.maximum(tops[0], tops[1]), tops[2])
    fade = [jnp.exp2(t - top) for t in tops]
    total = sum(fade[g] * sum_buf[g : g + 1, :] for g in range(3))
    mix = sum(fade[g] * mix_buf[g : g + 1, :] for g in range(3))
    inverse = 1.0 / total
    mix_buf[3:4, :] = mix * inverse
    for p in range(groups):
        norm_buf[p, 0:1, :] = fade[(p + 1) // 2] * inverse

    def pack_rows(g, n):
        lo = g[n * tile : n * tile + half]
        hi = g[n * tile + half : (n + 1) * tile]
        rlo = lo[:, LATENT:]
        rhi = hi[:, LATENT:]
        rlo = rlo + pltpu.roll(rlo, ROPE, 1)
        rhi = rhi + pltpu.roll(rhi, ROPE, 1)
        return lo[:, 0:LATENT], hi[:, 0:LATENT], jnp.where(lane_half < ROPE, rlo, rhi)

    for target in range(groups):
        k = lax.rem(target - i + groups, groups)
        place = k + (k // 2) * (5 - 2 * k)
        span_rows = pl.ds(pl.multiple_of(place * per_slot, per_slot), per_slot)

        def weigh(p, carry, place=place, span_rows=span_rows):
            span = pl.ds(pl.multiple_of(p * 256, 256), 256)
            w = e_buf[span_rows, span] * norm_buf[place, 0:1, span]
            w_buf[span_rows, span] = w.astype(bf)
            ds_buf[span_rows, span] = (w * ((dp_buf[span_rows, span] - mix_buf[3:4, span]) * scale)).astype(bf)
            return carry

        lax.fori_loop(0, rows // 256, weigh, 0, unroll=True)
        dsk = ds_buf[span_rows, :]
        wk = w_buf[span_rows, :]
        g_lat = lax.dot_general(dsk, qcat[:, 0:LATENT], natural, preferred_element_type=f32)
        g_lat = g_lat + lax.dot_general(wk, upcat[...], natural, preferred_element_type=f32)
        g_rot = lax.dot_general(dsk, qcat[:, LATENT:], natural, preferred_element_type=f32)
        g = jnp.concatenate([g_lat, g_rot], axis=1)
        for n in (5, 4, 3, 2, 1, 0):
            lo, hi, rot = pack_rows(g, n)
            if n == 0:
                gown[k, :, 0:LATENT] = lo
                gown[k, :, LATENT : 2 * LATENT] = hi
                gown[k, :, 2 * LATENT :] = rot
            else:
                gsend[k, n, :, 0:LATENT] = lo.astype(bf)
                gsend[k, n, :, LATENT : 2 * LATENT] = hi.astype(bf)
                gsend[k, n, :, 2 * LATENT :] = rot.astype(bf)
                launch(block_grad(k, n))

    outs = []
    lane_tok = lax.broadcasted_iota(jnp.int32, (tokens, 2 * ROPE), 1)
    for p in range(heads // 2):
        turned = []
        for h in (2 * p, 2 * p + 1):
            span = pl.ds(h * tokens, tokens)
            dq = lax.dot_general(ds_buf[:, span], kcat[...], (((0,), (0,)), ((), ())), preferred_element_type=f32)
            qc_ref[:, pl.ds(h * LATENT, LATENT)] = dq[:, 0:LATENT].astype(bf)
            turned.append(dq[:, LATENT:])
        rc_ref[:, pl.ds(p * 2 * ROPE, 2 * ROPE)] = jnp.where(lane_tok < ROPE, turned[0], turned[1]).astype(bf)

    for target in range(groups):
        k = lax.rem(target - i + groups, groups)
        total = gown[k]
        for n in range(1, nd):
            block_grad(k, n).wait_recv()
            total = total + gbuf[k, n].astype(f32)

        @pl.when(target == i)
        def _(total=total):
            rown[...] = total

        @pl.when(target != i)
        def _(total=total, k=k):
            rsend[k] = total.astype(bf)
            inner_grad(k).start()

    total = rown[...]
    for k in range(1, groups):
        inner_grad(groups - k).wait_recv()
        total = total + rbuf[k].astype(f32)
    lc_ref[0:half, :] = total[:, 0:LATENT]
    lc_ref[half:tile, :] = total[:, LATENT : 2 * LATENT]
    pc_ref[0:half, :] = total[:, 2 * LATENT : 2 * LATENT + ROPE]
    pc_ref[half:tile, :] = total[:, 2 * LATENT + ROPE :]
    for copy in sends:
        copy.wait_send()
    for k in range(1, groups):
        inner_grad(k).wait_send()


def place_results(*refs):
    copies = [pltpu.make_async_copy(refs[n], refs[4 + n], refs[8].at[n]) for n in range(4)]
    for copy in copies:
        copy.start()
    for copy in copies:
        copy.wait()


def per_device(query_latent, query_rotary, upstream, latent, key_rotary, pattern):
    blocks = lax.axis_size("blk")
    groups = lax.axis_size("inner")
    spacing = spacing_list(blocks)
    nd = len(spacing)
    scale = (NOPE + ROPE) ** (-0.5)
    tokens, width = query_latent.shape
    heads = width // LATENT
    rows = heads * tokens
    tile = latent.shape[0]
    half = tile // 2
    packed = 2 * (LATENT + ROPE)
    keys = nd * groups * tile
    vmem = pl.BlockSpec(memory_space=pltpu.VMEM)
    hbm = pl.BlockSpec(memory_space=pltpu.HBM)
    bf, f32 = jnp.bfloat16, jnp.float32
    dma = pltpu.SemaphoreType.DMA
    outs = pl.pallas_call(
        functools.partial(kernel, blocks, groups, spacing, scale),
        out_shape=(
            pltpu.VMEM(query_latent.shape, bf),
            pltpu.VMEM(query_rotary.shape, bf),
            pltpu.VMEM(latent.shape, f32),
            pltpu.VMEM(key_rotary.shape, f32),
        ),
        in_specs=[hbm] * 6,
        out_specs=(vmem, vmem, vmem, vmem),
        scratch_shapes=[
            pltpu.VMEM((rows, LATENT + 2 * ROPE), bf),
            pltpu.VMEM((rows, LATENT), bf),
            pltpu.VMEM((LATENT + 2 * ROPE, rows), bf),
            pltpu.VMEM((LATENT, rows), bf),
            pltpu.VMEM(query_rotary.shape, bf),
            pltpu.VMEM(latent.shape, bf),
            pltpu.VMEM(key_rotary.shape, bf),
            pltpu.SMEM(pattern.shape, jnp.int32),
            pltpu.VMEM((groups, nd, half, packed), bf),
            pltpu.VMEM((keys, LATENT + 2 * ROPE), bf),
            pltpu.VMEM((keys, rows), f32),
            pltpu.VMEM((keys, rows), f32),
            pltpu.VMEM((keys, rows), bf),
            pltpu.VMEM((keys, rows), bf),
            pltpu.VMEM((8, rows), f32),
            pltpu.VMEM((8, rows), f32),
            pltpu.VMEM((8, rows), f32),
            pltpu.VMEM((groups, 8, rows), f32),
            pltpu.VMEM((groups, nd, half, packed), bf),
            pltpu.VMEM((groups, half, packed), f32),
            pltpu.VMEM((groups, nd, half, packed), bf),
            pltpu.VMEM((groups, half, packed), bf),
            pltpu.VMEM((half, packed), f32),
            pltpu.VMEM((groups, half, packed), bf),
            dma((3,)),
            dma((1 + 2 * heads,)),
            dma((6,)),
            dma((6,)),
            dma((groups, nd)),
            dma((groups, nd)),
            dma((groups, nd)),
            dma((groups, nd)),
            dma((groups,)),
            dma((groups,)),
        ],
        compiler_params=pltpu.CompilerParams(
            collective_id=0, has_side_effects=True, vmem_limit_bytes=60 * 1024 * 1024
        ),
        cost_estimate=pl.CostEstimate(flops=4_300_000_000, bytes_accessed=4_000_000, transcendentals=800_000),
    )(query_latent, query_rotary, upstream, latent, key_rotary, pattern)
    return pl.pallas_call(
        place_results,
        out_shape=tuple(jax.ShapeDtypeStruct(x.shape, x.dtype) for x in outs),
        in_specs=[vmem] * 4,
        out_specs=tuple([hbm] * 4),
        scratch_shapes=[dma((4,))],
        compiler_params=pltpu.CompilerParams(vmem_limit_bytes=1024 * 1024),
    )(*outs)


def solution(mesh):
    in_specs = (
        P("blk", "inner"),
        P("blk", "inner"),
        P("blk", "inner"),
        P(("blk", "inner"), None),
        P(("blk", "inner"), None),
        P("blk", None),
    )
    out_specs = (
        P("blk", "inner"),
        P("blk", "inner"),
        P(("blk", "inner"), None),
        P(("blk", "inner"), None),
    )
    return jax.shard_map(
        per_device, mesh=mesh, in_specs=in_specs, out_specs=out_specs, check_vma=False
    )
```
